32 devices in a mesh: dom: 2 (over core), rep: 16 (over z, y, x).
Axes of the slice: x: 2, y: 2, z: 4, core: 2. Of those that a mesh axis runs over, the one named last changes fastest.
Arguments:
- cells: int32 [3, 524288], P(None, ('dom', 'rep')), may hold values from 0 to 191, as said below
- offsets: float32 [3, 524288], P(None, ('dom', 'rep')), may hold values from 0 to 1
- displacements: float32 [3, 524288], P(None, ('dom', 'rep')), may hold values from -1 to 1
- block_split: int32 [16384], P(('dom', 'rep')), may hold values from 8 to 24
- fields: float32 [2, 4, 36864], P(None, 'dom'), may hold values from -12 to 12
- crossing: int32 [32, 2, 16], P(('dom', 'rep')), may hold values from 0 to 511, as said below
- crossing_counts: int32 [32, 2], P(('dom', 'rep')), may hold values from 0 to 16, as said below
Outputs:
- new_offsets: float32 [3, 524288], P(None, ('dom', 'rep'))
- density: float32 [2, 4, 36864], P(None, 'dom', 'rep')
- arrivals: float32 [2, 3, 16384], P(None, None, ('dom', 'rep'))
The draws below stay inside these ranges and needn't reach their ends.
Inputs may be any that keep to these rules, and one draw needn't show every extreme that they name: x and y cells 0 to 191, z the layer 0 to 1 within the bead's domain; consecutive beads of a chain lie at most one cell apart along each direction (x and y periodically). `crossing`: the 32 entries of one device are distinct chain indices of that device. `crossing_counts`: the used slots are the first ones.
All inputs are finite; a program needn't handle non-finite values.
Results may differ from the reference program's by a relative error of at most 0.0003.
Values sent between devices are 32-bit elements; how exact they have to be, the bound alone decides.
A program may use at most 192 MiB of HBM per device.

```python
import jax
import jax.numpy as jnp
from jax import lax

GRID = 192
LZ = 2
NB = 32
CH_DEV = 512
MIG = 16
NZ = 4
CHAINS = 16384
BEADS = 524288
N_DOM = 2
N_REP = 16


def draw_cells(key, part):
    key = jax.random.fold_in(key, 11)
    devices = N_DOM * N_REP
    anchor_key, stride_key = jax.random.split(key)
    limits = jnp.array([GRID, GRID, LZ], jnp.int32).reshape(3, 1, 1, 1)
    anchor = jax.random.randint(anchor_key, (3, devices, 1, CH_DEV), 0, 1 << 20) % limits
    strides = jax.random.randint(stride_key, (3, devices, NB - 1, CH_DEV), -1, 2)
    walked = anchor + jnp.concatenate([jnp.zeros((3, devices, 1, CH_DEV), jnp.int32), jnp.cumsum(strides, axis=2)], axis=2)
    plane_cells = walked[:2] % GRID
    depth_cells = jnp.clip(walked[2:], 0, LZ - 1)
    return jnp.concatenate([plane_cells, depth_cells], axis=0).reshape(3, -1).astype(jnp.int32)


def draw_crossing(key, part):
    key = jax.random.fold_in(key, 37)
    device_keys = jax.random.split(key, N_DOM * N_REP)
    picks = jax.vmap(lambda device_key: jax.random.permutation(device_key, CH_DEV)[:2 * MIG])(device_keys)
    return picks.reshape(-1, 2, MIG).astype(jnp.int32)


def draw_crossing_counts(key, part):
    key = jax.random.fold_in(key, 23)
    slot_total = N_DOM * N_REP * 2
    value_key, first_key, second_key = jax.random.split(key, 3)
    values = jax.random.randint(value_key, (slot_total,), 0, MIG + 1)
    first = jax.random.randint(first_key, (), 0, slot_total)
    second = (first + 1 + jax.random.randint(second_key, (), 0, slot_total - 1)) % slot_total
    values = values.at[first].set(MIG).at[second].set(0)
    return values.reshape(-1, 2).astype(jnp.int32)


def place_ends(entries, stream_key, low, largest):
    longest = entries.shape.index(max(entries.shape))
    spots = []
    for shift in (0, 1):
        where = [jax.random.randint(jax.random.fold_in(stream_key, axis), (), 0, length) for axis, length in enumerate(entries.shape)]
        where[longest] = (where[longest] + shift) % entries.shape[longest]
        spots.append(tuple(where))
    return entries.at[spots[0]].set(low).at[spots[1]].set(largest)


def block_scale(stream_key, dims, cuts, low, top_value):
    loudness, own = 1.0, jax.random.fold_in(stream_key, 6)
    for dim, parts in cuts:
        draws = jnp.exp(jax.random.uniform(jax.random.fold_in(own, dim), (parts,), jnp.float32, low / len(cuts), top_value / len(cuts)))
        loudness = loudness * jnp.repeat(draws, dims[dim] // parts).reshape([-1 if axis == dim else 1 for axis in range(len(dims))])
    return loudness


def normal_values(stream_key, dims, spread, bound, pieces=(), held_as=jnp.bfloat16):
    result = spread * jax.random.normal(stream_key, dims, jnp.float32)
    if pieces:
        result = result * block_scale(stream_key, dims, pieces, -0.22, 0.18)
    return jnp.clip(result, -bound, bound).astype(held_as)


def setup_inputs(seed: int = 0) -> dict:
    key_of = jax.random.split(jax.random.key(seed), 8)
    return {
        "cells": draw_cells(jax.random.fold_in(key_of[7], 71), 0),
        "offsets": jnp.clip(1.0 * jax.random.uniform(key_of[1], (3, BEADS), jnp.float32) ** block_scale(key_of[1], (3, BEADS), ((1, 32),), -0.2, 0.2), 0.0, 1.0),
        "displacements": normal_values(key_of[2], (3, BEADS), 0.2, 1.0, ((1, 32),), jnp.float32),
        "block_split": place_ends(jax.random.randint(key_of[3], (CHAINS,), NB // 4, 3 * NB // 4 + 1), jax.random.fold_in(key_of[3], 1), NB // 4, (3 * NB // 4 + 1) - 1).astype(jnp.int32),
        "fields": normal_values(key_of[4], (2, NZ, GRID * GRID), 2.0, 12.0, ((1, 2),), jnp.float32),
        "crossing": draw_crossing(jax.random.fold_in(key_of[7], 71), 0),
        "crossing_counts": draw_crossing_counts(jax.random.fold_in(key_of[7], 71), 0),
    }


MOBILITY = 0.1


def wrap_gap(stride_gap, period):
    return (stride_gap + period // 2) % period - period // 2


def bond_force(cell_rows, offset_rows):
    stride_gap = cell_rows[:, 1:] - cell_rows[:, :-1]
    plane_gap = wrap_gap(stride_gap[:2], GRID)
    stride_gap = jnp.concatenate([plane_gap, stride_gap[2:]], axis=0).astype(jnp.float32)
    stride_gap = stride_gap + (offset_rows[:, 1:] - offset_rows[:, :-1])
    zeros_row = jnp.zeros_like(stride_gap[:, :1])
    return jnp.concatenate([stride_gap, zeros_row], axis=1) - jnp.concatenate([zeros_row, stride_gap], axis=1)


def field_forces(padded):
    interior = padded[:, 1:-1]
    layer_count = interior.shape[1]
    force_z = (padded[:, :-2] - padded[:, 2:]) * 0.5
    square = interior.reshape(2, layer_count, GRID, GRID)
    force_x = ((jnp.roll(square, 1, 2) - jnp.roll(square, -1, 2)) * 0.5).reshape(2, layer_count, GRID * GRID)
    force_y = ((jnp.roll(square, 1, 3) - jnp.roll(square, -1, 3)) * 0.5).reshape(2, layer_count, GRID * GRID)
    return jnp.stack([force_x, force_y, force_z]).reshape(3, -1)


def move_beads(cell_rows, offset_rows, displace_rows, split_rows, forces, layer_base, layer_count):
    bead_count = cell_rows.shape[1]
    positions_along = jnp.arange(bead_count, dtype=jnp.int32)[:, None]
    species = (positions_along >= split_rows[None, :]).astype(jnp.int32)
    plane_index = cell_rows[0] * GRID + cell_rows[1]
    layer_of = cell_rows[2] + layer_base
    lookup = species * (layer_count * GRID * GRID) + layer_of * (GRID * GRID) + plane_index
    field_push = forces[:, lookup]
    shifted = offset_rows + MOBILITY * (bond_force(cell_rows, offset_rows) + field_push) + displace_rows
    return shifted, species, plane_index, layer_of


def deposit(shifted, species, plane_index, layer_of, upper_layer, layer_count):
    upper_share = jnp.clip(shifted[2], 0.0, 1.0)
    base_index = species * (layer_count * GRID * GRID) + plane_index
    lower_index = (base_index + layer_of * (GRID * GRID)).reshape(-1)
    upper_index = (base_index + upper_layer * (GRID * GRID)).reshape(-1)
    all_index = jnp.concatenate([lower_index, upper_index])
    all_weight = jnp.concatenate([(1.0 - upper_share).reshape(-1), upper_share.reshape(-1)])
    grid_sum = jnp.zeros((2 * layer_count * GRID * GRID,), jnp.float32)
    return grid_sum.at[all_index].add(all_weight)


def crossing_rows(cell_rows, shifted, chosen, count_used, lift_by):
    position = cell_rows.astype(jnp.float32) + shifted
    picked = jnp.take(position, chosen, axis=2)
    picked = picked.at[2].add(lift_by)
    kept_mask = (jnp.arange(chosen.shape[0], dtype=jnp.int32) < count_used).astype(jnp.float32)
    return (picked * kept_mask).reshape(3, -1)


def reference(cells, offsets, displacements, block_split, fields, crossing, crossing_counts):
    devices = N_DOM * N_REP
    layers_all = LZ * N_DOM

    def per_device(array):
        return jnp.moveaxis(array.reshape(3, devices, NB, CH_DEV), 1, 0)

    padded = jnp.concatenate([fields[:, -1:], fields, fields[:, :1]], axis=1)
    forces = field_forces(padded)

    def one_device(density_sum, slices_in):
        cell_rows, offset_rows, displace_rows, split_rows, chosen, count_pair, device_number = slices_in
        layer_base = (device_number // N_REP) * LZ
        shifted, species, plane_index, layer_of = move_beads(cell_rows, offset_rows, displace_rows, split_rows, forces, layer_base, layers_all)
        density_sum = density_sum + deposit(shifted, species, plane_index, layer_of, (layer_of + 1) % layers_all, layers_all)
        rising = crossing_rows(cell_rows, shifted, chosen[0], count_pair[0], -float(LZ))
        falling = crossing_rows(cell_rows, shifted, chosen[1], count_pair[1], float(LZ))
        return density_sum, (shifted.reshape(3, -1), rising, falling)

    slices_all = (per_device(cells), per_device(offsets), per_device(displacements), block_split.reshape(devices, CH_DEV), crossing, crossing_counts, jnp.arange(devices, dtype=jnp.int32))
    start_sum = jnp.zeros((2 * layers_all * GRID * GRID,), jnp.float32)
    density_sum, outputs = lax.scan(one_device, start_sum, slices_all)
    shifted_all, rising, falling = outputs
    density_scale = GRID * GRID * LZ / (N_REP * CH_DEV * NB)
    density = density_sum.reshape(2, layers_all, GRID * GRID) * density_scale
    new_offsets = jnp.moveaxis(shifted_all, 0, 1).reshape(3, -1)
    slot_size = rising.shape[-1]
    rising = jnp.roll(rising.reshape(N_DOM, N_REP, 3, slot_size), 1, 0).reshape(devices, 3, slot_size)
    falling = jnp.roll(falling.reshape(N_DOM, N_REP, 3, slot_size), -1, 0).reshape(devices, 3, slot_size)
    arrivals = jnp.moveaxis(jnp.stack([rising, falling]), 1, 2).reshape(2, 3, -1)
    return new_offsets, density, arrivals
```

```python
import functools

import jax
import jax.numpy as jnp
from jax import lax
from jax.experimental import pallas as pl
from jax.experimental.pallas import tpu as pltpu
from jax.sharding import PartitionSpec as P

GRID = 192


MOBILITY = 0.1


def step_kernel(
    layers, beads, chains, slots, group, scale,
    count_ref, cells_ref, offsets_ref, displace_ref, split_ref, field_ref, low_ref, high_ref,
    cross_ref, out_ref, grid_ref, carry_ref, picked_ref,
    table_hi, table_lo, hot, weights, total, position,
):
    planes = 2 * layers
    keys = planes * GRID

    for s in range(2):
        for layer in range(layers):
            q = s * layers + layer
            w = field_ref[q]
            below = low_ref[s] if layer == 0 else field_ref[q - 1]
            above = high_ref[s] if layer == layers - 1 else field_ref[q + 1]
            back_x = jnp.concatenate([w[GRID - 1 :], w[: GRID - 1]], axis=0)
            ahead_x = jnp.concatenate([w[1:], w[:1]], axis=0)
            back_y = jnp.concatenate([w[:, GRID - 1 :], w[:, : GRID - 1]], axis=1)
            ahead_y = jnp.concatenate([w[:, 1:], w[:, :1]], axis=1)
            forces = (back_x - ahead_x, back_y - ahead_y, below - above)
            for k, force in enumerate(forces):
                force = force * 0.5
                top = force.astype(jnp.bfloat16)
                rest = (force - top.astype(jnp.float32)).astype(jnp.bfloat16)
                table_hi[k * GRID : (k + 1) * GRID, q * GRID : (q + 1) * GRID] = top
                table_lo[k * GRID : (k + 1) * GRID, q * GRID : (q + 1) * GRID] = rest

    total[...] = jnp.zeros_like(total)
    key_rows = lax.broadcasted_iota(jnp.int32, (keys, chains), 0)
    x_rows = lax.broadcasted_iota(jnp.int32, (GRID, chains), 0)

    def gap(cell_a, off_a, cell_b, off_b):
        d = cell_b - cell_a
        d = jnp.where(d > GRID // 2 - 1, d - GRID, jnp.where(d < -(GRID // 2), d + GRID, d))
        return d.astype(jnp.float32) + (off_b - off_a)

    def columns(j):
        return pl.ds(pl.multiple_of(j * chains, 128), chains)

    @pl.loop(0, beads // group)
    def _(g):
        for jj in range(group):
            j = g * group + jj
            here = columns(j)
            after = columns(jnp.minimum(j + 1, beads - 1))
            before = columns(jnp.maximum(j - 1, 0))
            cell, off = cells_ref[:, here], offsets_ref[:, here]
            gap_after = gap(cell, off, cells_ref[:, after], offsets_ref[:, after])
            gap_before = gap(cells_ref[:, before], offsets_ref[:, before], cell, off)
            bond = gap_after - gap_before
            species = (split_ref[...] <= j).astype(jnp.int32)
            key = (species * layers + cell[2:3]) * GRID + cell[1:2]
            chosen = jnp.where(key_rows == key, 1.0, 0.0).astype(jnp.bfloat16)
            hot[:, jj * chains : (jj + 1) * chains] = chosen
            found = jnp.dot(table_hi[...], chosen, preferred_element_type=jnp.float32)
            found += jnp.dot(table_lo[...], chosen, preferred_element_type=jnp.float32)
            at_x = x_rows == cell[0:1]
            push = [
                jnp.sum(
                    jnp.where(at_x, found[k * GRID : (k + 1) * GRID], 0.0), axis=0, keepdims=True
                )
                for k in range(3)
            ]
            moved = off + MOBILITY * (bond + jnp.concatenate(push, axis=0)) + displace_ref[:, here]
            out_ref[:, here] = moved
            place = cell.astype(jnp.float32) + moved
            for k in range(3):
                position[pl.ds(k * beads + j, 1), :] = place[k : k + 1]
            t = jnp.clip(moved[2:3], 0.0, 1.0)
            top = t.astype(jnp.bfloat16).astype(jnp.float32)
            here_w = slice(jj * chains, (jj + 1) * chains)
            weights[0:GRID, here_w] = jnp.where(at_x, 1.0, 0.0).astype(jnp.bfloat16)
            weights[GRID : 2 * GRID, here_w] = jnp.where(at_x, top, 0.0).astype(jnp.bfloat16)
            weights[2 * GRID :, here_w] = jnp.where(at_x, t - top, 0.0).astype(jnp.bfloat16)
        total[...] += lax.dot_general(
            weights[...], hot[...], (((1,), (1,)), ((), ())), preferred_element_type=jnp.float32
        )

    ones = total[0:GRID]
    upper = total[GRID : 2 * GRID] + total[2 * GRID :]
    lower = (ones - upper) * scale
    upper = upper * scale
    for s in range(2):
        for layer in range(layers):
            q = s * layers + layer
            part = lower[:, q * GRID : (q + 1) * GRID]
            if layer > 0:
                part = part + upper[:, (q - 1) * GRID : q * GRID]
            grid_ref[q] = part
        last = s * layers + layers - 1
        carry_ref[s] = upper[:, last * GRID : (last + 1) * GRID]

    chain_rows = lax.broadcasted_iota(jnp.int32, (chains, 2 * slots), 0)
    pick = jnp.where(chain_rows == cross_ref[...], 1.0, 0.0)
    picked = jnp.dot(
        position[...], pick, precision=lax.Precision.HIGHEST, preferred_element_type=jnp.float32
    )
    rows = lax.broadcasted_iota(jnp.int32, picked.shape, 0)
    slot = lax.broadcasted_iota(jnp.int32, picked.shape, 1)
    upward = slot < slots
    lift = jnp.where(upward, -float(layers), float(layers))
    picked = jnp.where(rows >= 2 * beads, picked + lift, picked)
    limit = jnp.where(upward, count_ref[0, 0], slots + count_ref[0, 1])
    picked_ref[...] = jnp.where(slot < limit, picked, 0.0)


def shifted(value, axis, steps):
    count = lax.axis_size(axis)
    return lax.ppermute(value, axis, [(i, (i + steps) % count) for i in range(count)])


def shards(cells, offsets, displacements, block_split, fields, crossing, crossing_counts):
    chains = block_split.shape[0]
    beads = cells.shape[1] // chains
    layers = fields.shape[1]
    slots = crossing.shape[2]
    plane = GRID * GRID
    group = 4
    scale = plane * layers / (lax.axis_size("rep") * chains * beads)
    square = fields.reshape(2, layers, GRID, GRID)
    low = shifted(square[:, layers - 1], "dom", 1)
    high = shifted(square[:, 0], "dom", -1)
    vmem = pl.BlockSpec(memory_space=pltpu.VMEM)
    new_offsets, grid, carry, picked = pl.pallas_call(
        functools.partial(step_kernel, layers, beads, chains, slots, group, scale),
        out_shape=(
            jax.ShapeDtypeStruct(offsets.shape, jnp.float32),
            jax.ShapeDtypeStruct((2 * layers, GRID, GRID), jnp.float32),
            jax.ShapeDtypeStruct((2, GRID, GRID), jnp.float32),
            jax.ShapeDtypeStruct((3 * beads, 2 * slots), jnp.float32),
        ),
        in_specs=[pl.BlockSpec(memory_space=pltpu.SMEM)] + [vmem] * 8,
        out_specs=(vmem,) * 4,
        scratch_shapes=[
            pltpu.VMEM((3 * GRID, 2 * layers * GRID), jnp.bfloat16),
            pltpu.VMEM((3 * GRID, 2 * layers * GRID), jnp.bfloat16),
            pltpu.VMEM((2 * layers * GRID, group * chains), jnp.bfloat16),
            pltpu.VMEM((3 * GRID, group * chains), jnp.bfloat16),
            pltpu.VMEM((3 * GRID, 2 * layers * GRID), jnp.float32),
            pltpu.VMEM((3 * beads, chains), jnp.float32),
        ],
        compiler_params=pltpu.CompilerParams(vmem_limit_bytes=48 * 1024 * 1024),
    )(
        crossing_counts,
        cells,
        offsets,
        displacements,
        block_split.reshape(1, chains),
        square.reshape(2 * layers, GRID, GRID),
        low,
        high,
        crossing.reshape(1, 2 * slots),
    )
    grid = grid.reshape(2, layers, GRID, GRID)
    carried = shifted(carry, "dom", 1)
    grid = jnp.concatenate([grid[:, :1] + carried[:, None], grid[:, 1:]], axis=1)
    density = lax.psum_scatter(
        grid.reshape(2, layers, plane), "rep", scatter_dimension=2, tiled=True
    )
    arrived_up = shifted(picked[:, :slots].reshape(3, -1), "dom", 1)
    arrived_down = shifted(picked[:, slots:].reshape(3, -1), "dom", -1)
    return new_offsets, density, jnp.stack([arrived_up, arrived_down])


def solution(mesh):
    in_specs = (
        P(None, ("dom", "rep")),
        P(None, ("dom", "rep")),
        P(None, ("dom", "rep")),
        P(("dom", "rep")),
        P(None, "dom", None),
        P(("dom", "rep"), None, None),
        P(("dom", "rep"), None),
    )
    out_specs = (P(None, ("dom", "rep")), P(None, "dom", "rep"), P(None, None, ("dom", "rep")))
    return jax.shard_map(shards, mesh=mesh, in_specs=in_specs, out_specs=out_specs, check_vma=False)
```

```python
import functools

import jax
import jax.numpy as jnp
from jax import lax
from jax.experimental import pallas as pl
from jax.experimental.pallas import tpu as pltpu
from jax.sharding import PartitionSpec as P

GRID = 192


MOBILITY = 0.1


def step_kernel(
    layers, beads, chains, slots, group, scale,
    count_ref, cells_ref, offsets_ref, displace_ref, split_ref, field_ref, low_ref, high_ref,
    cross_ref, out_ref, grid_ref, carry_ref, picked_ref,
    table_hi, table_lo, hot, weights, total, position,
):
    planes = 2 * layers
    keys = planes * GRID

    for s in range(2):
        for layer in range(layers):
            p, q = s * layers + layer, layer * 2 + s
            w = field_ref[p]
            below = low_ref[s] if layer == 0 else field_ref[p - 1]
            above = high_ref[s] if layer == layers - 1 else field_ref[p + 1]
            back_x = jnp.concatenate([w[GRID - 1 :], w[: GRID - 1]], axis=0)
            ahead_x = jnp.concatenate([w[1:], w[:1]], axis=0)
            back_y = jnp.concatenate([w[:, GRID - 1 :], w[:, : GRID - 1]], axis=1)
            ahead_y = jnp.concatenate([w[:, 1:], w[:, :1]], axis=1)
            forces = (back_x - ahead_x, back_y - ahead_y, below - above)
            for k, force in enumerate(forces):
                force = force * 0.5
                top = force.astype(jnp.bfloat16)
                rest = (force - top.astype(jnp.float32)).astype(jnp.bfloat16)
                table_hi[k * GRID : (k + 1) * GRID, q * GRID : (q + 1) * GRID] = top
                table_lo[k * GRID : (k + 1) * GRID, q * GRID : (q + 1) * GRID] = rest

    total[...] = jnp.zeros_like(total)
    key_rows = lax.broadcasted_iota(jnp.int32, (keys, chains), 0)
    x_rows = lax.broadcasted_iota(jnp.int32, (GRID, chains), 0)

    def gap(cell_a, off_a, cell_b, off_b):
        d = cell_b - cell_a
        d = jnp.where(d > GRID // 2 - 1, d - GRID, jnp.where(d < -(GRID // 2), d + GRID, d))
        return d.astype(jnp.float32) + (off_b - off_a)

    def columns(j):
        return pl.ds(pl.multiple_of(j * chains, 128), chains)

    @pl.loop(0, beads // group)
    def _(g):
        for jj in range(group):
            j = g * group + jj
            here = columns(j)
            after = columns(jnp.minimum(j + 1, beads - 1))
            before = columns(jnp.maximum(j - 1, 0))
            cell, off = cells_ref[:, here], offsets_ref[:, here]
            gap_after = gap(cell, off, cells_ref[:, after], offsets_ref[:, after])
            gap_before = gap(cells_ref[:, before], offsets_ref[:, before], cell, off)
            bond = gap_after - gap_before
            species = (split_ref[...] <= j).astype(jnp.int32)
            key = (cell[2:3] * 2 + species) * GRID + cell[1:2]
            chosen = jnp.where(key_rows == key, 1.0, 0.0).astype(jnp.bfloat16)
            hot[:, jj * chains : (jj + 1) * chains] = chosen
            found = jnp.dot(table_hi[...], chosen, preferred_element_type=jnp.float32)
            found += jnp.dot(table_lo[...], chosen, preferred_element_type=jnp.float32)
            at_x = x_rows == cell[0:1]
            push = [
                jnp.sum(
                    jnp.where(at_x, found[k * GRID : (k + 1) * GRID], 0.0), axis=0, keepdims=True
                )
                for k in range(3)
            ]
            moved = off + MOBILITY * (bond + jnp.concatenate(push, axis=0)) + displace_ref[:, here]
            out_ref[:, here] = moved
            place = cell.astype(jnp.float32) + moved
            for k in range(3):
                position[pl.ds(k * beads + j, 1), :] = place[k : k + 1]
            t = jnp.clip(moved[2:3], 0.0, 1.0)
            top = t.astype(jnp.bfloat16).astype(jnp.float32)
            here_w = slice(jj * chains, (jj + 1) * chains)
            weights[0:GRID, here_w] = jnp.where(at_x, 1.0, 0.0).astype(jnp.bfloat16)
            weights[GRID : 2 * GRID, here_w] = jnp.where(at_x, top, 0.0).astype(jnp.bfloat16)
            weights[2 * GRID :, here_w] = jnp.where(at_x, t - top, 0.0).astype(jnp.bfloat16)
        total[...] += lax.dot_general(
            weights[...], hot[...], (((1,), (1,)), ((), ())), preferred_element_type=jnp.float32
        )

    ones = total[0:GRID]
    upper = total[GRID : 2 * GRID] + total[2 * GRID :]
    lower = (ones - upper) * scale
    upper = upper * scale
    pair = 2 * GRID
    shares, rows = carry_ref.shape[0], carry_ref.shape[1]
    for layer in range(layers):
        part = lower[:, layer * pair : (layer + 1) * pair]
        if layer > 0:
            part = part + upper[:, (layer - 1) * pair : layer * pair]
        for r in range(shares):
            grid_ref[r, layer] = part[r * rows : (r + 1) * rows]
    for r in range(shares):
        carry_ref[r] = upper[r * rows : (r + 1) * rows, (layers - 1) * pair :]

    chain_rows = lax.broadcasted_iota(jnp.int32, (chains, 2 * slots), 0)
    pick = jnp.where(chain_rows == cross_ref[...], 1.0, 0.0)
    picked = jnp.dot(
        position[...], pick, precision=lax.Precision.HIGHEST, preferred_element_type=jnp.float32
    )
    element = lax.broadcasted_iota(jnp.int32, picked.shape, 0)
    slot = lax.broadcasted_iota(jnp.int32, picked.shape, 1)
    upward = slot < slots
    lift = jnp.where(upward, -float(layers), float(layers))
    picked = jnp.where(element >= 2 * beads, picked + lift, picked)
    limit = jnp.where(upward, count_ref[0, 0], slots + count_ref[0, 1])
    picked = jnp.where(slot < limit, picked, 0.0)
    picked_ref[0] = picked[:, :slots]
    picked_ref[1] = picked[:, slots:]


def exchange_kernel(
    count, domains, layers,
    grid_ref, carry_ref, picked_ref, density_ref, arrivals_ref,
    base, carried, crossed, slots, side_send, side_recv, send, recv,
):
    rep, dom = lax.axis_index("rep"), lax.axis_index("dom")
    above, below = lax.rem(dom + 1, domains), lax.rem(dom + domains - 1, domains)
    mesh_id = pl.DeviceIdType.MESH

    barrier = pltpu.get_barrier_semaphore()
    for side in (above, below):
        pl.semaphore_signal(barrier, inc=1, device_id=(side, rep), device_id_type=mesh_id)

    @pl.loop(1, count)
    def _(o):
        target = lax.rem(rep + o, count)
        pl.semaphore_signal(barrier, inc=1, device_id=(dom, target), device_id_type=mesh_id)

    pl.semaphore_wait(barrier, count + 1)

    def side_copy(source, landing, number, side):
        return pltpu.make_async_remote_copy(
            src_ref=source, dst_ref=landing,
            send_sem=side_send.at[number], recv_sem=side_recv.at[number],
            device_id=(side, rep), device_id_type=mesh_id,
        )

    carry_copy = side_copy(carry_ref, carried, 0, above)
    up_copy = side_copy(picked_ref.at[0], crossed.at[0], 1, above)
    down_copy = side_copy(picked_ref.at[1], crossed.at[1], 2, below)
    carry_copy.start()

    def block_copy(layer, o):
        target = lax.rem(rep + o, count)
        source = base.at[target] if layer == 0 else grid_ref.at[target, layer]
        return pltpu.make_async_remote_copy(
            src_ref=source, dst_ref=slots.at[layer, o],
            send_sem=send.at[layer, o], recv_sem=recv.at[layer, o],
            device_id=(dom, target), device_id_type=mesh_id,
        )

    order = list(range(1, layers)) + [0]
    for layer in order:
        if layer == 0:
            carry_copy.wait()
            base[...] = grid_ref[:, 0] + carried[...]

        @pl.loop(1, count)
        def _(o):
            block_copy(layer, o).start()

    up_copy.start()
    down_copy.start()

    for layer in order:
        own = base[rep] if layer == 0 else grid_ref[rep, layer]

        def gather_in(o, summed):
            block_copy(layer, o).wait()
            return summed + slots[layer, o]

        summed = lax.fori_loop(1, count, gather_in, own)
        density_ref[0, layer] = summed[:, :GRID]
        density_ref[1, layer] = summed[:, GRID:]

    up_copy.wait()
    down_copy.wait()
    arrivals_ref[...] = crossed[...]


def shifted(value, axis, steps):
    count = lax.axis_size(axis)
    return lax.ppermute(value, axis, [(i, (i + steps) % count) for i in range(count)])


def shards(cells, offsets, displacements, block_split, fields, crossing, crossing_counts):
    chains = block_split.shape[0]
    beads = cells.shape[1] // chains
    layers = fields.shape[1]
    slots = crossing.shape[2]
    plane = GRID * GRID
    group = 4
    scale = plane * layers / (lax.axis_size("rep") * chains * beads)
    square = fields.reshape(2, layers, GRID, GRID)
    low = shifted(square[:, layers - 1], "dom", 1)
    high = shifted(square[:, 0], "dom", -1)
    count, domains = lax.axis_size("rep"), lax.axis_size("dom")
    rows = GRID // count
    vmem = pl.BlockSpec(memory_space=pltpu.VMEM)
    new_offsets, grid, carry, picked = pl.pallas_call(
        functools.partial(step_kernel, layers, beads, chains, slots, group, scale),
        out_shape=(
            jax.ShapeDtypeStruct(offsets.shape, jnp.float32),
            jax.ShapeDtypeStruct((count, layers, rows, 2 * GRID), jnp.float32),
            jax.ShapeDtypeStruct((count, rows, 2 * GRID), jnp.float32),
            jax.ShapeDtypeStruct((2, 3 * beads, slots), jnp.float32),
        ),
        in_specs=[pl.BlockSpec(memory_space=pltpu.SMEM)] + [vmem] * 8,
        out_specs=(vmem,) * 4,
        scratch_shapes=[
            pltpu.VMEM((3 * GRID, 2 * layers * GRID), jnp.bfloat16),
            pltpu.VMEM((3 * GRID, 2 * layers * GRID), jnp.bfloat16),
            pltpu.VMEM((2 * layers * GRID, group * chains), jnp.bfloat16),
            pltpu.VMEM((3 * GRID, group * chains), jnp.bfloat16),
            pltpu.VMEM((3 * GRID, 2 * layers * GRID), jnp.float32),
            pltpu.VMEM((3 * beads, chains), jnp.float32),
        ],
        compiler_params=pltpu.CompilerParams(vmem_limit_bytes=48 * 1024 * 1024),
    )(
        crossing_counts,
        cells,
        offsets,
        displacements,
        block_split.reshape(1, chains),
        square.reshape(2 * layers, GRID, GRID),
        low,
        high,
        crossing.reshape(1, 2 * slots),
    )
    density, arrivals = pl.pallas_call(
        functools.partial(exchange_kernel, count, domains, layers),
        out_shape=(
            jax.ShapeDtypeStruct((2, layers, rows, GRID), jnp.float32),
            jax.ShapeDtypeStruct((2, 3 * beads, slots), jnp.float32),
        ),
        in_specs=[vmem] * 3,
        out_specs=(vmem,) * 2,
        scratch_shapes=[
            pltpu.VMEM((count, rows, 2 * GRID), jnp.float32),
            pltpu.VMEM((count, rows, 2 * GRID), jnp.float32),
            pltpu.VMEM((2, 3 * beads, slots), jnp.float32),
            pltpu.VMEM((layers, count, rows, 2 * GRID), jnp.float32),
            pltpu.SemaphoreType.DMA((3,)),
            pltpu.SemaphoreType.DMA((3,)),
            pltpu.SemaphoreType.DMA((layers, count)),
            pltpu.SemaphoreType.DMA((layers, count)),
        ],
        compiler_params=pltpu.CompilerParams(
            collective_id=0, has_side_effects=True, vmem_limit_bytes=16 * 1024 * 1024
        ),
    )(grid, carry, picked)
    return (
        new_offsets,
        density.reshape(2, layers, rows * GRID),
        arrivals.reshape(2, 3, beads * slots),
    )


def solution(mesh):
    in_specs = (
        P(None, ("dom", "rep")),
        P(None, ("dom", "rep")),
        P(None, ("dom", "rep")),
        P(("dom", "rep")),
        P(None, "dom", None),
        P(("dom", "rep"), None, None),
        P(("dom", "rep"), None),
    )
    out_specs = (P(None, ("dom", "rep")), P(None, "dom", "rep"), P(None, None, ("dom", "rep")))
    return jax.shard_map(shards, mesh=mesh, in_specs=in_specs, out_specs=out_specs, check_vma=False)
```

```python
import functools

import jax
import jax.numpy as jnp
from jax import lax
from jax.experimental import pallas as pl
from jax.experimental.pallas import tpu as pltpu
from jax.sharding import PartitionSpec as P

GRID = 192


MOBILITY = 0.1


SPLIT_MIN, SPLIT_MAX = 8, 24


def step_kernel(
    layers, beads, chains, slots, group, scale,
    count_ref, cells_ref, offsets_ref, displace_ref, split_ref, field_ref, low_ref, high_ref,
    cross_ref, out_ref, first_ref, second_ref, carry_ref, picked_ref,
    table, hot, weights, total, position,
):
    keys = layers * GRID
    pair = 2 * GRID

    for s in range(2):
        for layer in range(layers):
            p = s * layers + layer
            w = field_ref[p]
            below = low_ref[s] if layer == 0 else field_ref[p - 1]
            above = high_ref[s] if layer == layers - 1 else field_ref[p + 1]
            back_x = jnp.concatenate([w[GRID - 1 :], w[: GRID - 1]], axis=0)
            ahead_x = jnp.concatenate([w[1:], w[:1]], axis=0)
            back_y = jnp.concatenate([w[:, GRID - 1 :], w[:, : GRID - 1]], axis=1)
            ahead_y = jnp.concatenate([w[:, 1:], w[:, :1]], axis=1)
            forces = (back_x - ahead_x, back_y - ahead_y, below - above)
            for k, force in enumerate(forces):
                force = force * 0.5
                top = force.astype(jnp.bfloat16)
                rest = (force - top.astype(jnp.float32)).astype(jnp.bfloat16)
                here = slice(k * GRID, (k + 1) * GRID)
                table[s, here, layer * GRID : (layer + 1) * GRID] = top
                table[s, here, keys + layer * GRID : keys + (layer + 1) * GRID] = rest

    total[...] = jnp.zeros_like(total)
    key_rows = lax.broadcasted_iota(jnp.int32, (keys, chains), 0)
    x_rows = lax.broadcasted_iota(jnp.int32, (GRID, chains), 0)

    def gap(cell_a, off_a, cell_b, off_b):
        d = cell_b - cell_a
        d = jnp.where(d > GRID // 2 - 1, d - GRID, jnp.where(d < -(GRID // 2), d + GRID, d))
        return d.astype(jnp.float32) + (off_b - off_a)

    def columns(j):
        return pl.ds(pl.multiple_of(j * chains, 128), chains)

    def advance(g, kinds):
        for jj in range(group):
            j = g * group + jj
            here = columns(j)
            after = columns(jnp.minimum(j + 1, beads - 1))
            before = columns(jnp.maximum(j - 1, 0))
            cell, off = cells_ref[:, here], offsets_ref[:, here]
            gap_after = gap(cell, off, cells_ref[:, after], offsets_ref[:, after])
            gap_before = gap(cells_ref[:, before], offsets_ref[:, before], cell, off)
            bond = gap_after - gap_before
            key = cell[2:3] * GRID + cell[1:2]
            if len(kinds) > 1:
                species = (split_ref[...] <= j).astype(jnp.int32)
            found = None
            for at, kind in enumerate(kinds):
                own_key = key if len(kinds) == 1 else jnp.where(species == kind, key, -1)
                chosen = jnp.where(key_rows == own_key, 1.0, 0.0).astype(jnp.bfloat16)
                hot[at * keys : (at + 1) * keys, jj * chains : (jj + 1) * chains] = chosen
                product = jnp.dot(
                    table[kind],
                    jnp.concatenate([chosen, chosen], axis=0),
                    preferred_element_type=jnp.float32,
                )
                found = product if found is None else found + product
            at_x = x_rows == cell[0:1]
            push = [
                jnp.sum(
                    jnp.where(at_x, found[k * GRID : (k + 1) * GRID], 0.0), axis=0, keepdims=True
                )
                for k in range(3)
            ]
            moved = off + MOBILITY * (bond + jnp.concatenate(push, axis=0)) + displace_ref[:, here]
            out_ref[:, here] = moved
            place = cell.astype(jnp.float32) + moved
            for k in range(3):
                position[pl.ds(k * beads + j, 1), :] = place[k : k + 1]
            t = jnp.clip(moved[2:3], 0.0, 1.0)
            top = t.astype(jnp.bfloat16).astype(jnp.float32)
            here_w = slice(jj * chains, (jj + 1) * chains)
            weights[0:GRID, here_w] = jnp.where(at_x, 1.0, 0.0).astype(jnp.bfloat16)
            weights[GRID : 2 * GRID, here_w] = jnp.where(at_x, top, 0.0).astype(jnp.bfloat16)
            weights[2 * GRID :, here_w] = jnp.where(at_x, t - top, 0.0).astype(jnp.bfloat16)
        target = slice(kinds[0] * keys, (kinds[-1] + 1) * keys)
        total[:, target] += lax.dot_general(
            weights[...], hot[: len(kinds) * keys], (((1,), (1,)), ((), ())),
            preferred_element_type=jnp.float32,
        )

    head, tail = SPLIT_MIN // group, SPLIT_MAX // group
    for begin, end, kinds in ((0, head, (0,)), (head, tail, (0, 1)), (tail, beads // group, (1,))):
        pl.loop(begin, end)(functools.partial(advance, kinds=kinds))

    ones = total[0:GRID]
    upper = total[GRID : 2 * GRID] + total[2 * GRID :]
    lower = (ones - upper) * scale
    upper = upper * scale

    def both(counts, layer):
        return jnp.concatenate(
            [
                counts[:, s * keys + layer * GRID : s * keys + (layer + 1) * GRID]
                for s in range(2)
            ],
            axis=1,
        )

    bottom = both(lower, 0)
    top_layer = both(lower, 1) + both(upper, 0)
    leaving = both(upper, 1)
    shares, main = first_ref.shape[:2]
    spare = (second_ref.shape[1] - main) // 2
    rows = main + spare
    for r in range(shares):
        first_ref[r] = top_layer[r * rows : r * rows + main]
        second_ref[r, :rows] = bottom[r * rows : (r + 1) * rows]
        carry_ref[r, :rows] = leaving[r * rows : (r + 1) * rows]
        if spare:
            second_ref[r, rows:] = top_layer[r * rows + main : (r + 1) * rows]
            carry_ref[r, rows:] = jnp.zeros((spare, pair), jnp.float32)

    chain_rows = lax.broadcasted_iota(jnp.int32, (chains, 2 * slots), 0)
    pick = jnp.where(chain_rows == cross_ref[...], 1.0, 0.0)
    picked = jnp.dot(
        position[...], pick, precision=lax.Precision.HIGHEST, preferred_element_type=jnp.float32
    )
    element = lax.broadcasted_iota(jnp.int32, picked.shape, 0)
    slot = lax.broadcasted_iota(jnp.int32, picked.shape, 1)
    upward = slot < slots
    lift = jnp.where(upward, -float(layers), float(layers))
    picked = jnp.where(element >= 2 * beads, picked + lift, picked)
    limit = jnp.where(upward, count_ref[0, 0], slots + count_ref[0, 1])
    picked = jnp.where(slot < limit, picked, 0.0)
    picked_ref[0] = picked[:, :slots]
    picked_ref[1] = picked[:, slots:]


def exchange_kernel(
    count, domains,
    first_ref, second_ref, carry_ref, picked_ref, density_ref, arrivals_ref,
    base, carried, crossed, first_slots, second_slots, side_send, side_recv, send, recv,
):
    rep, dom = lax.axis_index("rep"), lax.axis_index("dom")
    above, below = lax.rem(dom + 1, domains), lax.rem(dom + domains - 1, domains)
    mesh_id = pl.DeviceIdType.MESH

    barrier = pltpu.get_barrier_semaphore()
    for side in (above, below):
        pl.semaphore_signal(barrier, inc=1, device_id=(side, rep), device_id_type=mesh_id)

    @pl.loop(1, count)
    def _(o):
        target = lax.rem(rep + o, count)
        pl.semaphore_signal(barrier, inc=1, device_id=(dom, target), device_id_type=mesh_id)

    pl.semaphore_wait(barrier, count + 1)

    def side_copy(source, landing, number, side):
        return pltpu.make_async_remote_copy(
            src_ref=source, dst_ref=landing,
            send_sem=side_send.at[number], recv_sem=side_recv.at[number],
            device_id=(side, rep), device_id_type=mesh_id,
        )

    carry_copy = side_copy(carry_ref, carried, 0, above)
    up_copy = side_copy(picked_ref.at[0], crossed.at[0], 1, above)
    down_copy = side_copy(picked_ref.at[1], crossed.at[1], 2, below)
    carry_copy.start()

    def block_copy(part, o):
        target = lax.rem(rep + o, count)
        source, landing = ((first_ref, first_slots), (base, second_slots))[part]
        return pltpu.make_async_remote_copy(
            src_ref=source.at[target], dst_ref=landing.at[o],
            send_sem=send.at[part, o], recv_sem=recv.at[part, o],
            device_id=(dom, target), device_id_type=mesh_id,
        )

    @pl.loop(1, count)
    def _(o):
        block_copy(0, o).start()

    carry_copy.wait()
    base[...] = second_ref[...] + carried[...]

    @pl.loop(1, count)
    def _(o):
        block_copy(1, o).start()

    up_copy.start()
    down_copy.start()

    def first_in(o, summed):
        block_copy(0, o).wait()
        return summed + first_slots[o]

    def second_in(o, summed):
        block_copy(1, o).wait()
        return summed + second_slots[o]

    first = lax.fori_loop(1, count, first_in, first_ref[rep])
    second = lax.fori_loop(1, count, second_in, base[rep])
    main = first.shape[0]
    rows = main + (second.shape[0] - main) // 2
    for s in range(2):
        lanes = slice(s * GRID, (s + 1) * GRID)
        density_ref[s, 0] = second[:rows, lanes]
        density_ref[s, 1, :main] = first[:, lanes]
        if rows > main:
            density_ref[s, 1, main:] = second[rows:, lanes]

    up_copy.wait()
    down_copy.wait()
    arrivals_ref[...] = crossed[...]


def shifted(value, axis, steps):
    count = lax.axis_size(axis)
    return lax.ppermute(value, axis, [(i, (i + steps) % count) for i in range(count)])


def shards(cells, offsets, displacements, block_split, fields, crossing, crossing_counts):
    chains = block_split.shape[0]
    beads = cells.shape[1] // chains
    layers = fields.shape[1]
    slots = crossing.shape[2]
    plane = GRID * GRID
    group = 4
    scale = plane * layers / (lax.axis_size("rep") * chains * beads)
    square = fields.reshape(2, layers, GRID, GRID)
    low = shifted(square[:, layers - 1], "dom", 1)
    high = shifted(square[:, 0], "dom", -1)
    count, domains = lax.axis_size("rep"), lax.axis_size("dom")
    rows = GRID // count
    spare = 4 if rows % 8 == 4 else 0
    first_shape = (count, rows - spare, 2 * GRID)
    second_shape = (count, rows + spare, 2 * GRID)
    vmem = pl.BlockSpec(memory_space=pltpu.VMEM)
    new_offsets, first, second, carry, picked = pl.pallas_call(
        functools.partial(step_kernel, layers, beads, chains, slots, group, scale),
        out_shape=(
            jax.ShapeDtypeStruct(offsets.shape, jnp.float32),
            jax.ShapeDtypeStruct(first_shape, jnp.float32),
            jax.ShapeDtypeStruct(second_shape, jnp.float32),
            jax.ShapeDtypeStruct(second_shape, jnp.float32),
            jax.ShapeDtypeStruct((2, 3 * beads, slots), jnp.float32),
        ),
        in_specs=[pl.BlockSpec(memory_space=pltpu.SMEM)] + [vmem] * 8,
        out_specs=(vmem,) * 5,
        scratch_shapes=[
            pltpu.VMEM((2, 3 * GRID, 2 * layers * GRID), jnp.bfloat16),
            pltpu.VMEM((2 * layers * GRID, group * chains), jnp.bfloat16),
            pltpu.VMEM((3 * GRID, group * chains), jnp.bfloat16),
            pltpu.VMEM((3 * GRID, 2 * layers * GRID), jnp.float32),
            pltpu.VMEM((3 * beads, chains), jnp.float32),
        ],
        compiler_params=pltpu.CompilerParams(vmem_limit_bytes=48 * 1024 * 1024),
    )(
        crossing_counts,
        cells,
        offsets,
        displacements,
        block_split.reshape(1, chains),
        square.reshape(2 * layers, GRID, GRID),
        low,
        high,
        crossing.reshape(1, 2 * slots),
    )
    density, arrivals = pl.pallas_call(
        functools.partial(exchange_kernel, count, domains),
        out_shape=(
            jax.ShapeDtypeStruct((2, layers, rows, GRID), jnp.float32),
            jax.ShapeDtypeStruct((2, 3 * beads, slots), jnp.float32),
        ),
        in_specs=[vmem] * 4,
        out_specs=(vmem,) * 2,
        scratch_shapes=[
            pltpu.VMEM(second_shape, jnp.float32),
            pltpu.VMEM(second_shape, jnp.float32),
            pltpu.VMEM((2, 3 * beads, slots), jnp.float32),
            pltpu.VMEM(first_shape, jnp.float32),
            pltpu.VMEM(second_shape, jnp.float32),
            pltpu.SemaphoreType.DMA((3,)),
            pltpu.SemaphoreType.DMA((3,)),
            pltpu.SemaphoreType.DMA((2, count)),
            pltpu.SemaphoreType.DMA((2, count)),
        ],
        compiler_params=pltpu.CompilerParams(
            collective_id=0, has_side_effects=True, vmem_limit_bytes=16 * 1024 * 1024
        ),
    )(first, second, carry, picked)
    return (
        new_offsets,
        density.reshape(2, layers, rows * GRID),
        arrivals.reshape(2, 3, beads * slots),
    )


def solution(mesh):
    in_specs = (
        P(None, ("dom", "rep")),
        P(None, ("dom", "rep")),
        P(None, ("dom", "rep")),
        P(("dom", "rep")),
        P(None, "dom", None),
        P(("dom", "rep"), None, None),
        P(("dom", "rep"), None),
    )
    out_specs = (P(None, ("dom", "rep")), P(None, "dom", "rep"), P(None, None, ("dom", "rep")))
    return jax.shard_map(shards, mesh=mesh, in_specs=in_specs, out_specs=out_specs, check_vma=False)
```

```python
import functools

import jax
import jax.numpy as jnp
from jax import lax
from jax.experimental import pallas as pl
from jax.experimental.pallas import tpu as pltpu
from jax.sharding import PartitionSpec as P

GRID = 192


MOBILITY = 0.1


SPLIT_MIN, SPLIT_MAX = 8, 24


def step_kernel(
    layers, beads, chains, slots, group, scale, count, domains,
    count_ref, cells_ref, offsets_ref, displace_ref, split_ref, field_ref, cross_ref,
    out_ref, density_ref, arrivals_ref,
    table, hot, weights, total, position, low_ref, high_ref,
    first_ref, second_ref, carry_ref, picked_ref,
    base, carried, crossed, first_slots, second_slots, side_send, side_recv, send, recv,
):
    keys = layers * GRID
    pair = 2 * GRID

    rep, dom = lax.axis_index("rep"), lax.axis_index("dom")
    above, below = lax.rem(dom + 1, domains), lax.rem(dom + domains - 1, domains)
    mesh_id = pl.DeviceIdType.MESH

    barrier = pltpu.get_barrier_semaphore()
    for side in (above, below):
        pl.semaphore_signal(barrier, inc=1, device_id=(side, rep), device_id_type=mesh_id)

    @pl.loop(1, count)
    def _(o):
        target = lax.rem(rep + o, count)
        pl.semaphore_signal(barrier, inc=1, device_id=(dom, target), device_id_type=mesh_id)

    pl.semaphore_wait(barrier, count + 1)

    def side_copy(source, landing, number, side):
        return pltpu.make_async_remote_copy(
            src_ref=source, dst_ref=landing,
            send_sem=side_send.at[number], recv_sem=side_recv.at[number],
            device_id=(side, rep), device_id_type=mesh_id,
        )

    halo_copies = []
    for s in range(2):
        top_w, bottom_w = field_ref.at[s * layers + layers - 1], field_ref.at[s * layers]
        halo_copies.append(side_copy(top_w, low_ref.at[s], 3 + s, above))
        halo_copies.append(side_copy(bottom_w, high_ref.at[s], 5 + s, below))
    for copy in halo_copies:
        copy.start()

    def tabulate(s, layer, k, force):
        force = force * 0.5
        top = force.astype(jnp.bfloat16)
        rest = (force - top.astype(jnp.float32)).astype(jnp.bfloat16)
        here = slice(k * GRID, (k + 1) * GRID)
        table[s, here, layer * GRID : (layer + 1) * GRID] = top
        table[s, here, keys + layer * GRID : keys + (layer + 1) * GRID] = rest

    for s in range(2):
        for layer in range(layers):
            w = field_ref[s * layers + layer]
            back_x = jnp.concatenate([w[GRID - 1 :], w[: GRID - 1]], axis=0)
            ahead_x = jnp.concatenate([w[1:], w[:1]], axis=0)
            back_y = jnp.concatenate([w[:, GRID - 1 :], w[:, : GRID - 1]], axis=1)
            ahead_y = jnp.concatenate([w[:, 1:], w[:, :1]], axis=1)
            tabulate(s, layer, 0, back_x - ahead_x)
            tabulate(s, layer, 1, back_y - ahead_y)

    for copy in halo_copies:
        copy.wait()
    for s in range(2):
        for layer in range(layers):
            p = s * layers + layer
            below_w = low_ref[s] if layer == 0 else field_ref[p - 1]
            above_w = high_ref[s] if layer == layers - 1 else field_ref[p + 1]
            tabulate(s, layer, 2, below_w - above_w)

    total[...] = jnp.zeros_like(total)
    key_rows = lax.broadcasted_iota(jnp.int32, (keys, chains), 0)
    x_rows = lax.broadcasted_iota(jnp.int32, (GRID, chains), 0)

    def gap(cell_a, off_a, cell_b, off_b):
        d = cell_b - cell_a
        d = jnp.where(d > GRID // 2 - 1, d - GRID, jnp.where(d < -(GRID // 2), d + GRID, d))
        return d.astype(jnp.float32) + (off_b - off_a)

    def columns(j):
        return pl.ds(pl.multiple_of(j * chains, 128), chains)

    def advance(g, kinds):
        for jj in range(group):
            j = g * group + jj
            here = columns(j)
            after = columns(jnp.minimum(j + 1, beads - 1))
            before = columns(jnp.maximum(j - 1, 0))
            cell, off = cells_ref[:, here], offsets_ref[:, here]
            gap_after = gap(cell, off, cells_ref[:, after], offsets_ref[:, after])
            gap_before = gap(cells_ref[:, before], offsets_ref[:, before], cell, off)
            bond = gap_after - gap_before
            key = cell[2:3] * GRID + cell[1:2]
            if len(kinds) > 1:
                species = (split_ref[...] <= j).astype(jnp.int32)
            found = None
            for at, kind in enumerate(kinds):
                own_key = key if len(kinds) == 1 else jnp.where(species == kind, key, -1)
                chosen = jnp.where(key_rows == own_key, 1.0, 0.0).astype(jnp.bfloat16)
                hot[at * keys : (at + 1) * keys, jj * chains : (jj + 1) * chains] = chosen
                product = jnp.dot(
                    table[kind],
                    jnp.concatenate([chosen, chosen], axis=0),
                    preferred_element_type=jnp.float32,
                )
                found = product if found is None else found + product
            at_x = x_rows == cell[0:1]
            push = [
                jnp.sum(
                    jnp.where(at_x, found[k * GRID : (k + 1) * GRID], 0.0), axis=0, keepdims=True
                )
                for k in range(3)
            ]
            moved = off + MOBILITY * (bond + jnp.concatenate(push, axis=0)) + displace_ref[:, here]
            out_ref[:, here] = moved
            place = cell.astype(jnp.float32) + moved
            for k in range(3):
                position[pl.ds(k * beads + j, 1), :] = place[k : k + 1]
            t = jnp.clip(moved[2:3], 0.0, 1.0)
            top = t.astype(jnp.bfloat16).astype(jnp.float32)
            here_w = slice(jj * chains, (jj + 1) * chains)
            weights[0:GRID, here_w] = jnp.where(at_x, 1.0, 0.0).astype(jnp.bfloat16)
            weights[GRID : 2 * GRID, here_w] = jnp.where(at_x, top, 0.0).astype(jnp.bfloat16)
            weights[2 * GRID :, here_w] = jnp.where(at_x, t - top, 0.0).astype(jnp.bfloat16)
        target = slice(kinds[0] * keys, (kinds[-1] + 1) * keys)
        total[:, target] += lax.dot_general(
            weights[...], hot[: len(kinds) * keys], (((1,), (1,)), ((), ())),
            preferred_element_type=jnp.float32,
        )

    head, tail = SPLIT_MIN // group, SPLIT_MAX // group
    for begin, end, kinds in ((0, head, (0,)), (head, tail, (0, 1)), (tail, beads // group, (1,))):
        pl.loop(begin, end)(functools.partial(advance, kinds=kinds))

    ones = total[0:GRID]
    upper = total[GRID : 2 * GRID] + total[2 * GRID :]
    lower = (ones - upper) * scale
    upper = upper * scale

    def both(counts, layer):
        return jnp.concatenate(
            [
                counts[:, s * keys + layer * GRID : s * keys + (layer + 1) * GRID]
                for s in range(2)
            ],
            axis=1,
        )

    bottom = both(lower, 0)
    top_layer = both(lower, 1) + both(upper, 0)
    leaving = both(upper, 1)
    shares, main = first_ref.shape[:2]
    spare = (second_ref.shape[1] - main) // 2
    rows = main + spare
    for r in range(shares):
        first_ref[r] = top_layer[r * rows : r * rows + main]
        second_ref[r, :rows] = bottom[r * rows : (r + 1) * rows]
        carry_ref[r, :rows] = leaving[r * rows : (r + 1) * rows]
        if spare:
            second_ref[r, rows:] = top_layer[r * rows + main : (r + 1) * rows]
            carry_ref[r, rows:] = jnp.zeros((spare, pair), jnp.float32)

    carry_copy = side_copy(carry_ref, carried, 0, above)
    up_copy = side_copy(picked_ref.at[0], crossed.at[0], 1, above)
    down_copy = side_copy(picked_ref.at[1], crossed.at[1], 2, below)
    carry_copy.start()

    def block_copy(part, o):
        target = lax.rem(rep + o, count)
        source, landing = ((first_ref, first_slots), (base, second_slots))[part]
        return pltpu.make_async_remote_copy(
            src_ref=source.at[target], dst_ref=landing.at[o],
            send_sem=send.at[part, o], recv_sem=recv.at[part, o],
            device_id=(dom, target), device_id_type=mesh_id,
        )

    @pl.loop(1, count)
    def _(o):
        block_copy(0, o).start()

    carry_copy.wait()
    base[...] = second_ref[...] + carried[...]

    @pl.loop(1, count)
    def _(o):
        block_copy(1, o).start()

    chain_rows = lax.broadcasted_iota(jnp.int32, (chains, 2 * slots), 0)
    pick = jnp.where(chain_rows == cross_ref[...], 1.0, 0.0)
    picked = jnp.dot(
        position[...], pick, precision=lax.Precision.HIGHEST, preferred_element_type=jnp.float32
    )
    element = lax.broadcasted_iota(jnp.int32, picked.shape, 0)
    slot = lax.broadcasted_iota(jnp.int32, picked.shape, 1)
    upward = slot < slots
    lift = jnp.where(upward, -float(layers), float(layers))
    picked = jnp.where(element >= 2 * beads, picked + lift, picked)
    limit = jnp.where(upward, count_ref[0, 0], slots + count_ref[0, 1])
    picked = jnp.where(slot < limit, picked, 0.0)
    picked_ref[0] = picked[:, :slots]
    picked_ref[1] = picked[:, slots:]

    up_copy.start()
    down_copy.start()

    def first_in(o, summed):
        block_copy(0, o).wait()
        return summed + first_slots[o]

    def second_in(o, summed):
        block_copy(1, o).wait()
        return summed + second_slots[o]

    first = lax.fori_loop(1, count, first_in, first_ref[rep])
    second = lax.fori_loop(1, count, second_in, base[rep])
    main = first.shape[0]
    rows = main + (second.shape[0] - main) // 2
    for s in range(2):
        lanes = slice(s * GRID, (s + 1) * GRID)
        density_ref[s, 0] = second[:rows, lanes]
        density_ref[s, 1, :main] = first[:, lanes]
        if rows > main:
            density_ref[s, 1, main:] = second[rows:, lanes]

    up_copy.wait()
    down_copy.wait()
    arrivals_ref[...] = crossed[...]


def shards(cells, offsets, displacements, block_split, fields, crossing, crossing_counts):
    chains = block_split.shape[0]
    beads = cells.shape[1] // chains
    layers = fields.shape[1]
    slots = crossing.shape[2]
    plane = GRID * GRID
    group = 4
    scale = plane * layers / (lax.axis_size("rep") * chains * beads)
    square = fields.reshape(2, layers, GRID, GRID)
    count, domains = lax.axis_size("rep"), lax.axis_size("dom")
    rows = GRID // count
    spare = 4 if rows % 8 == 4 else 0
    first_shape = (count, rows - spare, 2 * GRID)
    second_shape = (count, rows + spare, 2 * GRID)
    vmem = pl.BlockSpec(memory_space=pltpu.VMEM)
    new_offsets, density, arrivals = pl.pallas_call(
        functools.partial(
            step_kernel, layers, beads, chains, slots, group, scale, count, domains
        ),
        out_shape=(
            jax.ShapeDtypeStruct(offsets.shape, jnp.float32),
            jax.ShapeDtypeStruct((2, layers, rows, GRID), jnp.float32),
            jax.ShapeDtypeStruct((2, 3 * beads, slots), jnp.float32),
        ),
        in_specs=[pl.BlockSpec(memory_space=pltpu.SMEM)] + [vmem] * 6,
        out_specs=(vmem,) * 3,
        scratch_shapes=[
            pltpu.VMEM((2, 3 * GRID, 2 * layers * GRID), jnp.bfloat16),
            pltpu.VMEM((2 * layers * GRID, group * chains), jnp.bfloat16),
            pltpu.VMEM((3 * GRID, group * chains), jnp.bfloat16),
            pltpu.VMEM((3 * GRID, 2 * layers * GRID), jnp.float32),
            pltpu.VMEM((3 * beads, chains), jnp.float32),
            pltpu.VMEM((2, GRID, GRID), jnp.float32),
            pltpu.VMEM((2, GRID, GRID), jnp.float32),
            pltpu.VMEM(first_shape, jnp.float32),
            pltpu.VMEM(second_shape, jnp.float32),
            pltpu.VMEM(second_shape, jnp.float32),
            pltpu.VMEM((2, 3 * beads, slots), jnp.float32),
            pltpu.VMEM(second_shape, jnp.float32),
            pltpu.VMEM(second_shape, jnp.float32),
            pltpu.VMEM((2, 3 * beads, slots), jnp.float32),
            pltpu.VMEM(first_shape, jnp.float32),
            pltpu.VMEM(second_shape, jnp.float32),
            pltpu.SemaphoreType.DMA((7,)),
            pltpu.SemaphoreType.DMA((7,)),
            pltpu.SemaphoreType.DMA((2, count)),
            pltpu.SemaphoreType.DMA((2, count)),
        ],
        compiler_params=pltpu.CompilerParams(
            collective_id=0, has_side_effects=True, vmem_limit_bytes=48 * 1024 * 1024
        ),
    )(
        crossing_counts,
        cells,
        offsets,
        displacements,
        block_split.reshape(1, chains),
        square.reshape(2 * layers, GRID, GRID),
        crossing.reshape(1, 2 * slots),
    )
    return (
        new_offsets,
        density.reshape(2, layers, rows * GRID),
        arrivals.reshape(2, 3, beads * slots),
    )


def solution(mesh):
    in_specs = (
        P(None, ("dom", "rep")),
        P(None, ("dom", "rep")),
        P(None, ("dom", "rep")),
        P(("dom", "rep")),
        P(None, "dom", None),
        P(("dom", "rep"), None, None),
        P(("dom", "rep"), None),
    )
    out_specs = (P(None, ("dom", "rep")), P(None, "dom", "rep"), P(None, None, ("dom", "rep")))
    return jax.shard_map(shards, mesh=mesh, in_specs=in_specs, out_specs=out_specs, check_vma=False)
```

```python
import functools

import jax
import jax.numpy as jnp
from jax import lax
from jax.experimental import pallas as pl
from jax.experimental.pallas import tpu as pltpu
from jax.sharding import PartitionSpec as P

GRID = 192


MOBILITY = 0.1


SPLIT_MIN, SPLIT_MAX = 8, 24


def step_kernel(
    layers, beads, chains, slots, group, scale, count, domains,
    count_ref, cells_ref, offsets_ref, displace_ref, split_ref, field_ref, cross_ref,
    out_ref, density_ref, arrivals_ref,
    table, hot, weights, total, position, low_ref, high_ref,
    first_ref, second_ref, carry_ref, picked_ref,
    base, carried, crossed, first_slots, second_slots, side_send, side_recv, send, recv,
):
    keys = layers * GRID
    pair = 2 * GRID

    rep, dom = lax.axis_index("rep"), lax.axis_index("dom")
    above, below = lax.rem(dom + 1, domains), lax.rem(dom + domains - 1, domains)
    mesh_id = pl.DeviceIdType.MESH

    barrier = pltpu.get_barrier_semaphore()
    for side in (above, below):
        pl.semaphore_signal(barrier, inc=1, device_id=(side, rep), device_id_type=mesh_id)

    @pl.loop(1, count)
    def _(o):
        target = lax.rem(rep + o, count)
        pl.semaphore_signal(barrier, inc=1, device_id=(dom, target), device_id_type=mesh_id)

    def tabulate(s, layer, k, force):
        force = force * 0.5
        top = force.astype(jnp.bfloat16)
        rest = (force - top.astype(jnp.float32)).astype(jnp.bfloat16)
        here = slice(k * GRID, (k + 1) * GRID)
        table[s, here, layer * GRID : (layer + 1) * GRID] = top
        table[s, here, keys + layer * GRID : keys + (layer + 1) * GRID] = rest

    total[...] = jnp.zeros_like(total)
    for s in range(2):
        for layer in range(layers):
            w = field_ref[s * layers + layer]
            back_x = jnp.concatenate([w[GRID - 1 :], w[: GRID - 1]], axis=0)
            ahead_x = jnp.concatenate([w[1:], w[:1]], axis=0)
            tabulate(s, layer, 0, back_x - ahead_x)

    pl.semaphore_wait(barrier, count + 1)

    def side_copy(source, landing, number, side):
        return pltpu.make_async_remote_copy(
            src_ref=source, dst_ref=landing,
            send_sem=side_send.at[number], recv_sem=side_recv.at[number],
            device_id=(side, rep), device_id_type=mesh_id,
        )

    halo_copies = []
    for s in range(2):
        top_w, bottom_w = field_ref.at[s * layers + layers - 1], field_ref.at[s * layers]
        halo_copies.append(side_copy(top_w, low_ref.at[s], 3 + s, above))
        halo_copies.append(side_copy(bottom_w, high_ref.at[s], 5 + s, below))
    for copy in halo_copies:
        copy.start()

    for s in range(2):
        for layer in range(layers):
            w = field_ref[s * layers + layer]
            back_y = jnp.concatenate([w[:, GRID - 1 :], w[:, : GRID - 1]], axis=1)
            ahead_y = jnp.concatenate([w[:, 1:], w[:, :1]], axis=1)
            tabulate(s, layer, 1, back_y - ahead_y)

    for copy in halo_copies:
        copy.wait()
    for s in range(2):
        for layer in range(layers):
            p = s * layers + layer
            below_w = low_ref[s] if layer == 0 else field_ref[p - 1]
            above_w = high_ref[s] if layer == layers - 1 else field_ref[p + 1]
            tabulate(s, layer, 2, below_w - above_w)

    key_rows = lax.broadcasted_iota(jnp.int32, (keys, chains), 0)
    x_rows = lax.broadcasted_iota(jnp.int32, (GRID, chains), 0)

    def gap(cell_a, off_a, cell_b, off_b):
        d = cell_b - cell_a
        d = jnp.where(d > GRID // 2 - 1, d - GRID, jnp.where(d < -(GRID // 2), d + GRID, d))
        return d.astype(jnp.float32) + (off_b - off_a)

    def columns(j):
        return pl.ds(pl.multiple_of(j * chains, 128), chains)

    def advance(g, kinds):
        for jj in range(group):
            j = g * group + jj
            here = columns(j)
            after = columns(jnp.minimum(j + 1, beads - 1))
            before = columns(jnp.maximum(j - 1, 0))
            cell, off = cells_ref[:, here], offsets_ref[:, here]
            gap_after = gap(cell, off, cells_ref[:, after], offsets_ref[:, after])
            gap_before = gap(cells_ref[:, before], offsets_ref[:, before], cell, off)
            bond = gap_after - gap_before
            key = cell[2:3] * GRID + cell[1:2]
            if len(kinds) > 1:
                species = (split_ref[...] <= j).astype(jnp.int32)
            found = None
            for at, kind in enumerate(kinds):
                own_key = key if len(kinds) == 1 else jnp.where(species == kind, key, -1)
                chosen = jnp.where(key_rows == own_key, 1.0, 0.0).astype(jnp.bfloat16)
                hot[at * keys : (at + 1) * keys, jj * chains : (jj + 1) * chains] = chosen
                product = jnp.dot(
                    table[kind],
                    jnp.concatenate([chosen, chosen], axis=0),
                    preferred_element_type=jnp.float32,
                )
                found = product if found is None else found + product
            at_x = x_rows == cell[0:1]
            push = [
                jnp.sum(
                    jnp.where(at_x, found[k * GRID : (k + 1) * GRID], 0.0), axis=0, keepdims=True
                )
                for k in range(3)
            ]
            moved = off + MOBILITY * (bond + jnp.concatenate(push, axis=0)) + displace_ref[:, here]
            out_ref[:, here] = moved
            place = cell.astype(jnp.float32) + moved
            for k in range(3):
                position[pl.ds(k * beads + j, 1), :] = place[k : k + 1]
            t = jnp.clip(moved[2:3], 0.0, 1.0)
            top = t.astype(jnp.bfloat16).astype(jnp.float32)
            here_w = slice(jj * chains, (jj + 1) * chains)
            weights[0:GRID, here_w] = jnp.where(at_x, 1.0, 0.0).astype(jnp.bfloat16)
            weights[GRID : 2 * GRID, here_w] = jnp.where(at_x, top, 0.0).astype(jnp.bfloat16)
            weights[2 * GRID :, here_w] = jnp.where(at_x, t - top, 0.0).astype(jnp.bfloat16)
        target = slice(kinds[0] * keys, (kinds[-1] + 1) * keys)
        total[:, target] += lax.dot_general(
            weights[...], hot[: len(kinds) * keys], (((1,), (1,)), ((), ())),
            preferred_element_type=jnp.float32,
        )

    head, tail = SPLIT_MIN // group, SPLIT_MAX // group
    for begin, end, kinds in ((0, head, (0,)), (head, tail, (0, 1)), (tail, beads // group, (1,))):
        pl.loop(begin, end)(functools.partial(advance, kinds=kinds))

    ones = total[0:GRID]
    upper = total[GRID : 2 * GRID] + total[2 * GRID :]
    lower = (ones - upper) * scale
    upper = upper * scale

    def both(counts, layer):
        return jnp.concatenate(
            [
                counts[:, s * keys + layer * GRID : s * keys + (layer + 1) * GRID]
                for s in range(2)
            ],
            axis=1,
        )

    bottom = both(lower, 0)
    top_layer = both(lower, 1) + both(upper, 0)
    leaving = both(upper, 1)
    shares, main = first_ref.shape[:2]
    spare = (second_ref.shape[1] - main) // 2
    rows = main + spare
    for r in range(shares):
        first_ref[r] = top_layer[r * rows : r * rows + main]
        second_ref[r, :rows] = bottom[r * rows : (r + 1) * rows]
        carry_ref[r, :rows] = leaving[r * rows : (r + 1) * rows]
        if spare:
            second_ref[r, rows:] = top_layer[r * rows + main : (r + 1) * rows]
            carry_ref[r, rows:] = jnp.zeros((spare, pair), jnp.float32)

    carry_copy = side_copy(carry_ref, carried, 0, above)
    up_copy = side_copy(picked_ref.at[0], crossed.at[0], 1, above)
    down_copy = side_copy(picked_ref.at[1], crossed.at[1], 2, below)
    carry_copy.start()

    def block_copy(part, o):
        target = lax.rem(rep + o, count)
        source, landing = ((first_ref, first_slots), (base, second_slots))[part]
        return pltpu.make_async_remote_copy(
            src_ref=source.at[target], dst_ref=landing.at[o],
            send_sem=send.at[part, o], recv_sem=recv.at[part, o],
            device_id=(dom, target), device_id_type=mesh_id,
        )

    @pl.loop(1, count)
    def _(o):
        block_copy(0, o).start()

    carry_copy.wait()
    base[...] = second_ref[...] + carried[...]

    @pl.loop(1, count)
    def _(o):
        block_copy(1, o).start()

    chain_rows = lax.broadcasted_iota(jnp.int32, (chains, 2 * slots), 0)
    pick = jnp.where(chain_rows == cross_ref[...], 1.0, 0.0)
    picked = jnp.dot(
        position[...], pick, precision=lax.Precision.HIGHEST, preferred_element_type=jnp.float32
    )
    element = lax.broadcasted_iota(jnp.int32, picked.shape, 0)
    slot = lax.broadcasted_iota(jnp.int32, picked.shape, 1)
    upward = slot < slots
    lift = jnp.where(upward, -float(layers), float(layers))
    picked = jnp.where(element >= 2 * beads, picked + lift, picked)
    limit = jnp.where(upward, count_ref[0, 0], slots + count_ref[0, 1])
    picked = jnp.where(slot < limit, picked, 0.0)
    picked_ref[0] = picked[:, :slots]
    picked_ref[1] = picked[:, slots:]

    up_copy.start()
    down_copy.start()

    def first_in(o, summed):
        block_copy(0, o).wait()
        return summed + first_slots[o]

    def second_in(o, summed):
        block_copy(1, o).wait()
        return summed + second_slots[o]

    first = lax.fori_loop(1, count, first_in, first_ref[rep])
    second = lax.fori_loop(1, count, second_in, base[rep])
    main = first.shape[0]
    rows = main + (second.shape[0] - main) // 2
    for s in range(2):
        lanes = slice(s * GRID, (s + 1) * GRID)
        density_ref[s, 0] = second[:rows, lanes]
        density_ref[s, 1, :main] = first[:, lanes]
        if rows > main:
            density_ref[s, 1, main:] = second[rows:, lanes]

    up_copy.wait()
    down_copy.wait()
    arrivals_ref[...] = crossed[...]


def shards(cells, offsets, displacements, block_split, fields, crossing, crossing_counts):
    chains = block_split.shape[0]
    beads = cells.shape[1] // chains
    layers = fields.shape[1]
    slots = crossing.shape[2]
    plane = GRID * GRID
    group = 4
    scale = plane * layers / (lax.axis_size("rep") * chains * beads)
    square = fields.reshape(2, layers, GRID, GRID)
    count, domains = lax.axis_size("rep"), lax.axis_size("dom")
    rows = GRID // count
    spare = 4 if rows % 8 == 4 else 0
    first_shape = (count, rows - spare, 2 * GRID)
    second_shape = (count, rows + spare, 2 * GRID)
    vmem = pl.BlockSpec(memory_space=pltpu.VMEM)
    new_offsets, density, arrivals = pl.pallas_call(
        functools.partial(
            step_kernel, layers, beads, chains, slots, group, scale, count, domains
        ),
        out_shape=(
            jax.ShapeDtypeStruct(offsets.shape, jnp.float32),
            jax.ShapeDtypeStruct((2, layers, rows, GRID), jnp.float32),
            jax.ShapeDtypeStruct((2, 3 * beads, slots), jnp.float32),
        ),
        in_specs=[pl.BlockSpec(memory_space=pltpu.SMEM)] + [vmem] * 6,
        out_specs=(vmem,) * 3,
        scratch_shapes=[
            pltpu.VMEM((2, 3 * GRID, 2 * layers * GRID), jnp.bfloat16),
            pltpu.VMEM((2 * layers * GRID, group * chains), jnp.bfloat16),
            pltpu.VMEM((3 * GRID, group * chains), jnp.bfloat16),
            pltpu.VMEM((3 * GRID, 2 * layers * GRID), jnp.float32),
            pltpu.VMEM((3 * beads, chains), jnp.float32),
            pltpu.VMEM((2, GRID, GRID), jnp.float32),
            pltpu.VMEM((2, GRID, GRID), jnp.float32),
            pltpu.VMEM(first_shape, jnp.float32),
            pltpu.VMEM(second_shape, jnp.float32),
            pltpu.VMEM(second_shape, jnp.float32),
            pltpu.VMEM((2, 3 * beads, slots), jnp.float32),
            pltpu.VMEM(second_shape, jnp.float32),
            pltpu.VMEM(second_shape, jnp.float32),
            pltpu.VMEM((2, 3 * beads, slots), jnp.float32),
            pltpu.VMEM(first_shape, jnp.float32),
            pltpu.VMEM(second_shape, jnp.float32),
            pltpu.SemaphoreType.DMA((7,)),
            pltpu.SemaphoreType.DMA((7,)),
            pltpu.SemaphoreType.DMA((2, count)),
            pltpu.SemaphoreType.DMA((2, count)),
        ],
        compiler_params=pltpu.CompilerParams(
            collective_id=0, has_side_effects=True, vmem_limit_bytes=48 * 1024 * 1024
        ),
    )(
        crossing_counts,
        cells,
        offsets,
        displacements,
        block_split.reshape(1, chains),
        square.reshape(2 * layers, GRID, GRID),
        crossing.reshape(1, 2 * slots),
    )
    return (
        new_offsets,
        density.reshape(2, layers, rows * GRID),
        arrivals.reshape(2, 3, beads * slots),
    )


def solution(mesh):
    in_specs = (
        P(None, ("dom", "rep")),
        P(None, ("dom", "rep")),
        P(None, ("dom", "rep")),
        P(("dom", "rep")),
        P(None, "dom", None),
        P(("dom", "rep"), None, None),
        P(("dom", "rep"), None),
    )
    out_specs = (P(None, ("dom", "rep")), P(None, "dom", "rep"), P(None, None, ("dom", "rep")))
    return jax.shard_map(shards, mesh=mesh, in_specs=in_specs, out_specs=out_specs, check_vma=False)
```
